32 devices in a mesh: list: 8 (over z, x), help: 4 (over y, core).
Axes of the slice: x: 2, y: 2, z: 4, core: 2. Of those that a mesh axis runs over, the one named last changes fastest.
Arguments:
- members: bfloat16 [131072, 768], P(('list', 'help')), may hold values from -6 to 6
- owner: int32 [131072, 1], P(('list', 'help')), may hold values from 0 to 15; in each aligned block of 4096 rows (0 to 4095, 4096 to 8191, ...) at most 512 rows name the same one
- seed_label: int32 [131072], P(('list', 'help')), may hold values from 0 to 7
Outputs:
- assignments: float32 [8, 131072], P(None, ('list', 'help'))
- centroids: float32 [16, 8, 768], P('list')
The draws below stay inside these ranges and needn't reach their ends.
Inputs may be any that keep to these rules, and one draw needn't show every extreme that they name: `owner`: in each device's block of 4096 members no list is named by more than 512 of them, a bound that some block reaches; every list has members.
All inputs are finite; a program needn't handle non-finite values.
Results may differ from the reference program's by a relative error of at most 0.012.
The reference program's roundings to bfloat16 on the way count: a program that leaves them out, or rounds other values in their place, can miss the bound.
Values may be sent and summed in bfloat16 or wider, within the bound.
A program may use at most 128 MiB of HBM per device.

```python
import math
import jax
import jax.numpy as jnp
import numpy as np
from jax import lax

D = 768
K = 8
ITERS = 3
MEM_DEV = 4096
LISTS = 16
CAP = 512
MEMBERS = 131072


def draw_members(key, part):
    keys = jax.random.split(key, 1)
    values = jnp.clip(jax.random.normal(keys[0], (MEMBERS, D), jnp.float32), -6.0, 6.0)
    return values.astype(jnp.bfloat16)


def place_ends(drawn, rng, least, top_value):
    extent = drawn.shape
    spot = [jax.random.randint(jax.random.fold_in(rng, axis), (), 0, extent[axis]) for axis in range(len(extent))]
    drawn = drawn.at[tuple(spot)].set(least)
    longest = extent.index(max(extent))
    spot[longest] = (spot[longest] + 1) % extent[longest]
    return drawn.at[tuple(spot)].set(top_value)


def deal_out(rng, own, number, rows, count, top, limit, lean):
    sequence = jax.random.permutation(rng, count)
    packed, common = portions_of(count, rows * top, limit, lean, True), portions_of(count, rows * top, limit, lean, False)
    places = jnp.arange(count)

    def named(tallies, offset_by):
        used = int((tallies > 0).sum())
        fixed = max(1, used // 4)
        passed = fixed + (places - fixed + offset_by * (used - fixed)) % max(1, count - fixed)
        return jnp.zeros((count,), jnp.int32).at[sequence[jnp.where(places < fixed, places, passed)]].set(jnp.asarray(tallies, jnp.int32))

    tallies = jnp.where(number % 4 == 0, named(packed, number // 4), named(common, number - number // 4 - 1))
    mixed = jax.random.permutation(jax.random.fold_in(own, 3), count)
    giver, receiver = mixed[0:count // 2 * 2:2], mixed[1:count // 2 * 2:2]
    room = jnp.minimum(tallies[giver] - 1, limit - tallies[receiver]) // 2
    room = jnp.where((giver == sequence[0]) | (receiver == sequence[0]) | (tallies[receiver] == 0), 0, jnp.maximum(room, 0))
    passed = jax.random.randint(jax.random.fold_in(own, 4), (count // 2,), 0, 1 << 20) % (room + 1)
    tallies = tallies.at[giver].add(-passed).at[receiver].add(passed)
    labels = jnp.searchsorted(jnp.cumsum(tallies), jnp.arange(rows * top), side="right").astype(jnp.int32)
    listing = labels.reshape(top, rows).T
    listing = listing[jax.random.permutation(jax.random.fold_in(own, 1), rows)]
    offset_by = jax.random.randint(jax.random.fold_in(own, 2), (rows, 1), 0, top)
    return jnp.take_along_axis(listing, (jnp.arange(top)[None, :] + offset_by) % top, axis=1)


def portions_of(amount, total, limit, slope, full):
    portions = [(1 << 20) // math.isqrt(rank ** slope) + 1 for rank in range(1, amount + 1)]
    largest = limit if full else min(limit, max(-(-total // amount), total * portions[0] // sum(portions)))
    least = 1 if total - largest >= amount - 1 else 0
    holding, spare = [largest] + [least] * (amount - 1), total - largest - least * (amount - 1)
    while spare > 0:
        movable = [i for i in range(1, amount) if holding[i] < largest] or [i for i in range(1, amount) if holding[i] < limit]
        whole, remaining = sum([portions[i] for i in movable]), spare
        for i in movable:
            more = min(limit - holding[i], max(1, remaining * portions[i] // whole), spare)
            holding[i] = holding[i] + more
            spare = spare - more
    return np.array(holding)


def setup_inputs(seed: int = 0) -> dict:
    key_list = jax.random.split(jax.random.key(seed), 4)
    members = draw_members(jax.random.fold_in(key_list[3], 71), 0)
    owner_keys = jax.random.split(jax.random.fold_in(key_list[1], 1), MEMBERS // MEM_DEV)
    owner_turns = jax.random.permutation(jax.random.fold_in(key_list[1], 3), MEMBERS // MEM_DEV)
    owner = jax.vmap(lambda own, number: deal_out(jax.random.fold_in(key_list[1], 2), own, number, MEM_DEV, LISTS, 1, CAP, 2))(owner_keys, owner_turns).reshape((MEMBERS, 1))
    seed_label = place_ends(jax.random.randint(key_list[2], (MEMBERS,), 0, K), jax.random.fold_in(key_list[2], 1), 0, K - 1).astype(jnp.int32)
    return dict(members=members, owner=owner, seed_label=seed_label)


smoothing_heat_factor = 2.0


def soft_assign(block_vectors, tile_holder_entries, centers):
    center_bf = centers.astype(jnp.bfloat16)
    center_bf = lax.optimization_barrier(center_bf).astype(jnp.float32)
    centroid_magnitude_power = jnp.sum(centers * centers, axis=-1)
    chosen_subcentroid = center_bf[tile_holder_entries]
    separation_measures = jnp.einsum("yu,yru->yr", block_vectors.astype(jnp.float32), chosen_subcentroid, precision=lax.Precision.HIGHEST)
    membership_raw_preference = (2.0 * separation_measures - centroid_magnitude_power[tile_holder_entries]) / smoothing_heat_factor
    return jax.nn.softmax(membership_raw_preference, axis=-1)


def reference(members, owner, seed_label):
    own_ids = owner[:, 0]
    blocks = MEMBERS // MEM_DEV
    block_vectors = members.reshape(blocks, MEM_DEV, D)
    tile_holder_entries = own_ids.reshape(blocks, MEM_DEV)
    block_lab = seed_label.reshape(blocks, MEM_DEV)
    groups = jnp.arange(K, dtype=jnp.int32)

    def accumulate(centers, first):
        def step(carry, item):
            sums, totals = carry
            part_x, part_own, part_lab = item
            if first:
                weights = (part_lab[:, None] == groups[None, :]).astype(jnp.float32)
            else:
                weights = soft_assign(part_x, part_own, centers).astype(jnp.bfloat16)
                weights = lax.optimization_barrier(weights).astype(jnp.float32)
            seg_ids = (part_own[:, None] * K + groups[None, :]).reshape(-1).astype(jnp.int32)
            data = (weights[:, :, None] * part_x.astype(jnp.float32)[:, None, :]).reshape(-1, D)
            sums = sums + jax.ops.segment_sum(data, seg_ids, num_segments=LISTS * K)
            totals = totals + jax.ops.segment_sum(weights.reshape(-1), seg_ids, num_segments=LISTS * K)
            return (sums, totals), None

        start = (jnp.zeros((LISTS * K, D), jnp.float32), jnp.zeros((LISTS * K,), jnp.float32))
        (sums, totals), _ = lax.scan(step, start, (block_vectors, tile_holder_entries, block_lab))
        return (sums / (totals + 1.0)[:, None]).reshape(LISTS, K, D)

    centers = accumulate(jnp.zeros((LISTS, K, D), jnp.float32), True)
    for turn in range(ITERS):
        centers = accumulate(centers, False)
    final = lax.map(lambda item: soft_assign(item[0], item[1], centers), (block_vectors, tile_holder_entries))
    assignments = final.reshape(MEMBERS, K).T
    return assignments, centers
```

```python
import jax
import jax.numpy as jnp
from jax import lax
from jax.sharding import PartitionSpec as P

K = 8
ITERS = 3
LIST_DEV = 2
HEAT = 2.0


def local(members, owner, seed_label):
    rows, width = members.shape
    lists = lax.axis_size("list") * LIST_DEV
    own = owner[:, 0]
    hot = own[None, :] == jnp.arange(lists, dtype=jnp.int32)[:, None]
    seeds = seed_label[None, :] == jnp.arange(K, dtype=jnp.int32)[:, None]

    def update(weights):
        spread = jnp.where(hot[:, None, :], weights[None], 0).astype(jnp.bfloat16)
        spread = spread.reshape(lists * K, rows)
        sums = jnp.dot(spread, members, preferred_element_type=jnp.float32)
        totals = jnp.sum(spread.astype(jnp.float32), axis=1, keepdims=True)
        both = jnp.concatenate([sums, jnp.broadcast_to(totals, (lists * K, 128))], axis=1)
        both = lax.psum(both, ("list", "help"))
        return both[:, :width] / (both[:, width : width + 1] + 1.0)

    def assign(centers):
        inner = lax.dot_general(
            centers.astype(jnp.bfloat16),
            members,
            (((1,), (1,)), ((), ())),
            preferred_element_type=jnp.float32,
        )
        power = jnp.sum(centers * centers, axis=1, keepdims=True)
        logits = (2.0 * inner - power) / HEAT
        logits = jnp.sum(jnp.where(hot[:, None, :], logits.reshape(lists, K, rows), 0.0), axis=0)
        return jax.nn.softmax(logits, axis=0)

    centers = update(jnp.where(seeds, 1.0, 0.0))
    for _ in range(ITERS):
        centers = update(assign(centers))
    out = assign(centers)
    mine = lax.axis_index("list") * LIST_DEV * K
    own_centers = lax.dynamic_slice_in_dim(centers, mine, LIST_DEV * K, 0)
    return out, own_centers.reshape(LIST_DEV, K, width)


def solution(mesh):
    placed = (P(("list", "help"), None), P(("list", "help"), None), P(("list", "help")))
    return jax.shard_map(
        local,
        mesh=mesh,
        in_specs=placed,
        out_specs=(P(None, ("list", "help")), P("list", None, None)),
        check_vma=False,
    )
```

```python
import functools
import jax
import jax.numpy as jnp
from jax import lax
from jax.experimental import pallas as pl
from jax.experimental.pallas import tpu as pltpu
from jax.sharding import PartitionSpec as P

K = 8
ITERS = 3
LIST_DEV = 2
TILE = 1024
LANES = 128
MESH = pl.DeviceIdType.MESH


def kernel(
    n_list, n_help, members, own, seed, out, cent,
    acc, theirs, part, gathered, packs, table, power, mine, wide_table,
    sib_send, sib_recv, rs_send, rs_recv, ag_send, ag_recv, fin_send, fin_recv,
):
    rows, width = members.shape
    half = width // 2
    lists = n_list * LIST_DEV
    per_list = n_help // 2
    units = n_list * per_list
    i_list = lax.axis_index("list")
    i_help = lax.axis_index("help")
    core = lax.rem(i_help, 2)
    unit = i_list * per_list + i_help // 2

    def device_of(u, c):
        return (u // per_list, lax.rem(u, per_list) * 2 + c)

    sibling = (i_list, i_help + 1 - 2 * core)

    barrier = pltpu.get_barrier_semaphore()

    @pl.loop(1, units)
    def _(d):
        pl.semaphore_signal(
            barrier, inc=1, device_id=device_of(lax.rem(unit + d, units), core), device_id_type=MESH
        )

    for d in range(1, n_help):
        to = lax.rem(i_help + d, n_help)

        @pl.when(lax.rem(to, 2) != core)
        def _():
            pl.semaphore_signal(barrier, inc=1, device_id=(i_list, to), device_id_type=MESH)

    pl.semaphore_wait(barrier, units - 1 + per_list)

    def rs_copy(d, to, slot):
        return pltpu.make_async_remote_copy(
            src_ref=part.at[to], dst_ref=gathered.at[slot],
            send_sem=rs_send.at[d], recv_sem=rs_recv.at[d],
            device_id=device_of(to, core), device_id_type=MESH,
        )

    def ag_copy(d, to, slot):
        return pltpu.make_async_remote_copy(
            src_ref=packs.at[core, unit], dst_ref=packs.at[core, slot],
            send_sem=ag_send.at[d], recv_sem=ag_recv.at[d],
            device_id=device_of(to, core), device_id_type=MESH,
        )

    def assign(t):
        cols = pl.ds(pl.multiple_of(t * TILE, TILE), TILE)
        inner = lax.dot_general(
            table[...], members[cols, :], (((1,), (1,)), ((), ())),
            preferred_element_type=jnp.float32,
        )
        owner = jnp.broadcast_to(own[:, cols], (K, TILE))
        logit = jnp.zeros((K, TILE), jnp.float32)
        for l in range(lists):
            row = slice(l * K, (l + 1) * K)
            logit = jnp.where(owner == l, inner[row] - power[row, 0:1], logit)
        e = jnp.exp(logit - jnp.max(logit, axis=0, keepdims=True))
        return e / jnp.sum(e, axis=0, keepdims=True)

    def seeded(t):
        cols = pl.ds(pl.multiple_of(t * TILE, TILE), TILE)
        label = jnp.broadcast_to(seed[:, cols], (K, TILE))
        return jnp.where(label == lax.broadcasted_iota(jnp.int32, (K, TILE), 0), 1.0, 0.0)

    def accumulate(weigh):
        for h in range(2):
            acc[h] = jnp.zeros(acc.shape[1:], jnp.float32)

        @pl.loop(0, rows // TILE)
        def _(t):
            cols = pl.ds(pl.multiple_of(t * TILE, TILE), TILE)
            weight = weigh(t).astype(jnp.bfloat16).astype(jnp.float32)
            owner = jnp.broadcast_to(own[:, cols], (K, TILE))
            spread = jnp.concatenate(
                [jnp.where(owner == l, weight, 0.0) for l in range(lists)], axis=0
            )
            sums = jnp.dot(
                spread.astype(jnp.bfloat16), members[cols, :], preferred_element_type=jnp.float32
            )
            total = spread[:, :LANES]
            for j in range(1, TILE // LANES):
                total = total + spread[:, j * LANES : (j + 1) * LANES]
            for h in range(2):
                acc[h, :, :half] += sums[:, h * half : (h + 1) * half]
                acc[h, :, half:] += total

    def exchange():
        swap = pltpu.make_async_remote_copy(
            src_ref=acc.at[1 - core], dst_ref=theirs,
            send_sem=sib_send.at[0], recv_sem=sib_recv.at[0],
            device_id=sibling, device_id_type=MESH,
        )
        swap.start()
        swap.wait()
        both = acc[core] + theirs[...]
        part[...] = both.reshape(part.shape)

        @pl.loop(1, units)
        def _(d):
            rs_copy(d, lax.rem(unit + d, units), unit).start()

        gathered[unit] = part[unit]

        @pl.loop(1, units)
        def _(d):
            rs_copy(d, lax.rem(unit + d, units), lax.rem(unit + units - d, units)).wait()

        block = gathered[0]
        for u in range(1, units):
            block = block + gathered[u]
        total = jnp.sum(block[:, half:], axis=1, keepdims=True)
        centers = block[:, :half] / (total + 1.0)
        mine[...] = centers
        norm = 0.5 * jnp.sum(centers * centers, axis=1, keepdims=True)
        hi = norm.astype(jnp.bfloat16).astype(jnp.float32)
        mid = (norm - hi).astype(jnp.bfloat16).astype(jnp.float32)
        lo = norm - hi - mid
        lane = lax.broadcasted_iota(jnp.int32, (K, LANES), 1)
        tail = jnp.where(lane == 0, hi, jnp.where(lane == 1, mid, jnp.where(lane == 2, lo, 0.0)))
        wide = jnp.concatenate([centers, tail], axis=1)
        side = wide.shape[1] // 2
        packs[core, unit] = jnp.concatenate(
            [wide[:, :side], wide[:, side:]], axis=0
        ).astype(jnp.bfloat16)

        @pl.loop(1, units)
        def _(d):
            ag_copy(d, lax.rem(unit + d, units), unit).start()

        @pl.loop(1, units)
        def _(d):
            ag_copy(d, lax.rem(unit + d, units), lax.rem(unit + units - d, units)).wait()

        forward = pltpu.make_async_remote_copy(
            src_ref=packs.at[core], dst_ref=packs.at[core],
            send_sem=sib_send.at[1], recv_sem=sib_recv.at[1],
            device_id=sibling, device_id_type=MESH,
        )
        forward.start()
        forward.wait_send()
        pltpu.make_async_remote_copy(
            src_ref=packs.at[core], dst_ref=packs.at[1 - core],
            send_sem=sib_send.at[1], recv_sem=sib_recv.at[1],
            device_id=sibling, device_id_type=MESH,
        ).wait_recv()

        for l in range(lists):
            whole, norms = [], 0.0
            for h in range(2):
                got = packs[h, l].astype(jnp.float32)
                got = jnp.concatenate([got[:K], got[K:]], axis=1)
                whole.append(got[:, :half])
                norms = norms + jnp.sum(got[:, half:], axis=1, keepdims=True)
            power[l * K : (l + 1) * K, :] = jnp.broadcast_to(norms, (K, LANES))
            wide_table[l] = jnp.concatenate(whole, axis=1)
        table[...] = wide_table[...].reshape(table.shape).astype(jnp.bfloat16)

    accumulate(seeded)
    exchange()

    @pl.loop(0, ITERS)
    def _(turn):
        accumulate(assign)
        exchange()

    def fin_copy(d, slot):
        return pltpu.make_async_remote_copy(
            src_ref=mine, dst_ref=cent.at[slot],
            send_sem=fin_send.at[d], recv_sem=fin_recv.at[d],
            device_id=(i_list, lax.rem(i_help + d, n_help)), device_id_type=MESH,
        )

    for d in range(1, n_help):
        fin_copy(d, i_help).start()
    cent[i_help] = mine[...]

    @pl.loop(0, rows // TILE)
    def _(t):
        cols = pl.ds(pl.multiple_of(t * TILE, TILE), TILE)
        out[:, cols] = assign(t)

    for d in range(1, n_help):
        fin_copy(d, lax.rem(i_help + n_help - d, n_help)).wait()


def local(members, owner, seed_label):
    rows, width = members.shape
    n_list, n_help = lax.axis_size("list"), lax.axis_size("help")
    lists = n_list * LIST_DEV
    units = n_list * n_help // 2
    half = width // 2
    packed = half + LANES
    vmem = pl.BlockSpec(memory_space=pltpu.VMEM)
    dma = pltpu.SemaphoreType.DMA
    out, cent = pl.pallas_call(
        functools.partial(kernel, n_list, n_help),
        out_shape=(
            jax.ShapeDtypeStruct((K, rows), jnp.float32),
            jax.ShapeDtypeStruct((n_help, K, half), jnp.float32),
        ),
        in_specs=[vmem] * 3,
        out_specs=(vmem, vmem),
        scratch_shapes=[
            pltpu.VMEM((2, lists * K, packed), jnp.float32),
            pltpu.VMEM((lists * K, packed), jnp.float32),
            pltpu.VMEM((units, K, packed), jnp.float32),
            pltpu.VMEM((units, K, packed), jnp.float32),
            pltpu.VMEM((2, units, 2 * K, packed // 2), jnp.bfloat16),
            pltpu.VMEM((lists * K, width), jnp.bfloat16),
            pltpu.VMEM((lists * K, LANES), jnp.float32),
            pltpu.VMEM((K, half), jnp.float32),
            pltpu.VMEM((lists, K, width), jnp.float32),
            dma((2,)),
            dma((2,)),
            dma((units,)),
            dma((units,)),
            dma((units,)),
            dma((units,)),
            dma((n_help,)),
            dma((n_help,)),
        ],
        compiler_params=pltpu.CompilerParams(
            collective_id=0, has_side_effects=True, vmem_limit_bytes=48 * 1024 * 1024
        ),
    )(members, owner.reshape(1, rows), seed_label.reshape(1, rows))
    cent = cent.reshape(n_help // 2, 2, K, half).transpose(0, 2, 1, 3)
    return out, cent.reshape(LIST_DEV, K, width)


def solution(mesh):
    placed = (P(("list", "help"), None), P(("list", "help"), None), P(("list", "help")))
    return jax.shard_map(
        local,
        mesh=mesh,
        in_specs=placed,
        out_specs=(P(None, ("list", "help")), P("list", None, None)),
        check_vma=False,
    )
```

```python
import functools
import jax
import jax.numpy as jnp
from jax import lax
from jax.experimental import pallas as pl
from jax.experimental.pallas import tpu as pltpu
from jax.sharding import PartitionSpec as P

K = 8
ITERS = 3
LIST_DEV = 2
TILE = 1024
LANES = 128
MESH = pl.DeviceIdType.MESH


def kernel(
    n_list, n_help, source, own, seed, out, cent,
    members, weights, count, acc, theirs, part, gathered, packs, table, power, mine, wide_table,
    sib_send, sib_recv, rs_send, rs_recv, ag_send, ag_recv, fin_send, fin_recv, load_sem,
):
    rows, width = members.shape
    half = width // 2
    lists = n_list * LIST_DEV
    per_list = n_help // 2
    units = n_list * per_list
    i_list = lax.axis_index("list")
    i_help = lax.axis_index("help")
    core = lax.rem(i_help, 2)
    unit = i_list * per_list + i_help // 2

    def wrap(u):
        return jnp.where(u >= units, u - units, u)

    def device_of(u, c):
        return (u // per_list, lax.rem(u, per_list) * 2 + c)

    sibling = (i_list, i_help + 1 - 2 * core)

    load = pltpu.make_async_copy(source, members, load_sem)
    load.start()

    barrier = pltpu.get_barrier_semaphore()

    @pl.loop(1, units)
    def _(d):
        pl.semaphore_signal(
            barrier, inc=1, device_id=device_of(wrap(unit + d), core), device_id_type=MESH
        )

    for d in range(1, n_help):
        to = lax.rem(i_help + d, n_help)

        @pl.when(lax.rem(to, 2) != core)
        def _():
            pl.semaphore_signal(barrier, inc=1, device_id=(i_list, to), device_id_type=MESH)

    def arrive():
        load.wait()
        pl.semaphore_wait(barrier, units - 1 + per_list)

    def swap_copy(q):
        return pltpu.make_async_remote_copy(
            src_ref=acc.at[q, 1 - core], dst_ref=theirs.at[q],
            send_sem=sib_send.at[q], recv_sem=sib_recv.at[q],
            device_id=sibling, device_id_type=MESH,
        )

    def scatter(q):
        swap_copy(q).wait()
        part[q] = (acc[q, core] + theirs[q]).reshape(part.shape[1:])

        @pl.loop(1, units)
        def _(d):
            to = wrap(unit + d)
            pltpu.make_async_remote_copy(
                src_ref=part.at[q, to], dst_ref=gathered.at[q, unit],
                send_sem=rs_send.at[q], recv_sem=rs_recv.at[q],
                device_id=device_of(to, core), device_id_type=MESH,
            ).start()

        gathered[q, unit] = part[q, unit]

    def scatter_wait(q):
        pltpu.make_async_remote_copy(
            src_ref=part.at[q, : units - 1], dst_ref=gathered.at[q, : units - 1],
            send_sem=rs_send.at[q], recv_sem=rs_recv.at[q],
            device_id=sibling, device_id_type=MESH,
        ).wait()

    def assign(t):
        cols = pl.ds(pl.multiple_of(t * TILE, TILE), TILE)
        inner = lax.dot_general(
            table[...], members[cols, :], (((1,), (1,)), ((), ())),
            preferred_element_type=jnp.float32,
        )
        owner = jnp.broadcast_to(own[:, cols], (K, TILE))
        logit = jnp.zeros((K, TILE), jnp.float32)
        for l in range(lists):
            row = slice(l * K, (l + 1) * K)
            logit = jnp.where(owner == l, inner[row] - power[row, 0:1], logit)
        e = jnp.exp(logit - jnp.max(logit, axis=0, keepdims=True))
        return e / jnp.sum(e, axis=0, keepdims=True)

    def seeded(t):
        cols = pl.ds(pl.multiple_of(t * TILE, TILE), TILE)
        label = jnp.broadcast_to(seed[:, cols], (K, TILE))
        return jnp.where(label == lax.broadcasted_iota(jnp.int32, (K, TILE), 0), 1.0, 0.0)

    def weigh_all(weigh):
        count[...] = jnp.zeros_like(count)

        @pl.loop(0, rows // TILE)
        def _(t):
            cols = pl.ds(pl.multiple_of(t * TILE, TILE), TILE)
            weight = weigh(t).astype(jnp.bfloat16).astype(jnp.float32)
            owner = jnp.broadcast_to(own[:, cols], (K, TILE))
            spread = jnp.concatenate(
                [jnp.where(owner == l, weight, 0.0) for l in range(lists)], axis=0
            )
            weights[:, cols] = spread.astype(jnp.bfloat16)
            total = spread[:, :LANES]
            for j in range(1, TILE // LANES):
                total = total + spread[:, j * LANES : (j + 1) * LANES]
            count[...] += total

    def sum_columns(columns):
        return jnp.dot(weights[...], columns, preferred_element_type=jnp.float32)

    def exchange():
        ends = jnp.concatenate(
            [members[:, :LANES], members[:, half : half + LANES]], axis=1
        )
        sums = sum_columns(ends)
        for h in range(2):
            acc[0, h, :, :LANES] = sums[:, h * LANES : (h + 1) * LANES]
            acc[0, h, :, LANES:] = count[...]
        swap_copy(0).start()

        def rest(h):
            start = pl.multiple_of(h * half + LANES, LANES)
            acc[1, h] = sum_columns(members[:, pl.ds(start, half - LANES)])

        rest(1 - core)
        swap_copy(1).start()
        scatter(0)
        rest(core)
        scatter(1)
        scatter_wait(0)
        scatter_wait(1)

        block = [gathered[q, 0] for q in range(2)]
        for u in range(1, units):
            block = [block[q] + gathered[q, u] for q in range(2)]
        total = jnp.sum(block[0][:, LANES:], axis=1, keepdims=True)
        centers = jnp.concatenate([block[0][:, :LANES], block[1]], axis=1) / (total + 1.0)
        mine[...] = centers
        norm = 0.5 * jnp.sum(centers * centers, axis=1, keepdims=True)
        hi = norm.astype(jnp.bfloat16).astype(jnp.float32)
        mid = (norm - hi).astype(jnp.bfloat16).astype(jnp.float32)
        lo = norm - hi - mid
        lane = lax.broadcasted_iota(jnp.int32, (K, LANES), 1)
        tail = jnp.where(lane == 0, hi, jnp.where(lane == 1, mid, jnp.where(lane == 2, lo, 0.0)))
        wide = jnp.concatenate([centers, tail], axis=1)
        side = wide.shape[1] // 2
        packs[core, unit] = jnp.concatenate(
            [wide[:, :side], wide[:, side:]], axis=0
        ).astype(jnp.bfloat16)

        @pl.loop(1, units)
        def _(d):
            pltpu.make_async_remote_copy(
                src_ref=packs.at[core, unit], dst_ref=packs.at[core, unit],
                send_sem=ag_send.at[0], recv_sem=ag_recv.at[0],
                device_id=device_of(wrap(unit + d), core), device_id_type=MESH,
            ).start()

        pltpu.make_async_remote_copy(
            src_ref=packs.at[core, : units - 1], dst_ref=packs.at[core, : units - 1],
            send_sem=ag_send.at[0], recv_sem=ag_recv.at[0],
            device_id=sibling, device_id_type=MESH,
        ).wait()

        forward = pltpu.make_async_remote_copy(
            src_ref=packs.at[core], dst_ref=packs.at[core],
            send_sem=sib_send.at[2], recv_sem=sib_recv.at[2],
            device_id=sibling, device_id_type=MESH,
        )
        forward.start()
        forward.wait_send()
        pltpu.make_async_remote_copy(
            src_ref=packs.at[core], dst_ref=packs.at[1 - core],
            send_sem=sib_send.at[2], recv_sem=sib_recv.at[2],
            device_id=sibling, device_id_type=MESH,
        ).wait_recv()

        for l in range(lists):
            whole, norms = [], 0.0
            for h in range(2):
                got = packs[h, l].astype(jnp.float32)
                got = jnp.concatenate([got[:K], got[K:]], axis=1)
                whole.append(got[:, :half])
                norms = norms + jnp.sum(got[:, half:], axis=1, keepdims=True)
            power[l * K : (l + 1) * K, :] = jnp.broadcast_to(norms, (K, LANES))
            wide_table[l] = jnp.concatenate(whole, axis=1)
        table[...] = wide_table[...].reshape(table.shape).astype(jnp.bfloat16)

    weigh_all(seeded)
    arrive()
    exchange()

    @pl.loop(0, ITERS)
    def _(turn):
        weigh_all(assign)
        exchange()

    def fin_copy(d, slot):
        return pltpu.make_async_remote_copy(
            src_ref=mine, dst_ref=cent.at[slot],
            send_sem=fin_send.at[d], recv_sem=fin_recv.at[d],
            device_id=(i_list, lax.rem(i_help + d, n_help)), device_id_type=MESH,
        )

    for d in range(1, n_help):
        fin_copy(d, i_help).start()
    cent[i_help] = mine[...]

    @pl.loop(0, rows // TILE)
    def _(t):
        cols = pl.ds(pl.multiple_of(t * TILE, TILE), TILE)
        out[:, cols] = assign(t)

    for d in range(1, n_help):
        fin_copy(d, lax.rem(i_help + n_help - d, n_help)).wait()


def local(members, owner, seed_label):
    rows, width = members.shape
    n_list, n_help = lax.axis_size("list"), lax.axis_size("help")
    lists = n_list * LIST_DEV
    units = n_list * n_help // 2
    half = width // 2
    packed = half + LANES
    vmem = pl.BlockSpec(memory_space=pltpu.VMEM)
    dma = pltpu.SemaphoreType.DMA
    out, cent = pl.pallas_call(
        functools.partial(kernel, n_list, n_help),
        out_shape=(
            jax.ShapeDtypeStruct((K, rows), jnp.float32),
            jax.ShapeDtypeStruct((n_help, K, half), jnp.float32),
        ),
        in_specs=[pl.BlockSpec(memory_space=pl.ANY), vmem, vmem],
        out_specs=(vmem, vmem),
        scratch_shapes=[
            pltpu.VMEM((rows, width), jnp.bfloat16),
            pltpu.VMEM((lists * K, rows), jnp.bfloat16),
            pltpu.VMEM((lists * K, LANES), jnp.float32),
            pltpu.VMEM((2, 2, lists * K, half - LANES), jnp.float32),
            pltpu.VMEM((2, lists * K, half - LANES), jnp.float32),
            pltpu.VMEM((2, units, K, half - LANES), jnp.float32),
            pltpu.VMEM((2, units, K, half - LANES), jnp.float32),
            pltpu.VMEM((2, units, 2 * K, packed // 2), jnp.bfloat16),
            pltpu.VMEM((lists * K, width), jnp.bfloat16),
            pltpu.VMEM((lists * K, LANES), jnp.float32),
            pltpu.VMEM((K, half), jnp.float32),
            pltpu.VMEM((lists, K, width), jnp.float32),
            dma((3,)),
            dma((3,)),
            dma((2,)),
            dma((2,)),
            dma((1,)),
            dma((1,)),
            dma((n_help,)),
            dma((n_help,)),
            dma,
        ],
        compiler_params=pltpu.CompilerParams(
            collective_id=0, has_side_effects=True, vmem_limit_bytes=60 * 1024 * 1024
        ),
    )(members, owner.reshape(1, rows), seed_label.reshape(1, rows))
    cent = cent.reshape(n_help // 2, 2, K, half).transpose(0, 2, 1, 3)
    return out, cent.reshape(LIST_DEV, K, width)


def solution(mesh):
    placed = (P(("list", "help"), None), P(("list", "help"), None), P(("list", "help")))
    return jax.shard_map(
        local,
        mesh=mesh,
        in_specs=placed,
        out_specs=(P(None, ("list", "help")), P("list", None, None)),
        check_vma=False,
    )
```

```python
import functools
import jax
import jax.numpy as jnp
from jax import lax
from jax.experimental import pallas as pl
from jax.experimental.pallas import tpu as pltpu
from jax.sharding import PartitionSpec as P

K = 8
ITERS = 3
LIST_DEV = 2
TILE = 1024
LANES = 128
MESH = pl.DeviceIdType.MESH


def kernel(
    n_list, n_help, source, own, seed, out, cent,
    members, weights, count, acc, theirs, part, gathered, packs, table, power, mine, wide_table, logits,
    sib_send, sib_recv, rs_send, rs_recv, ag_send, ag_recv, fin_send, fin_recv, load_sem,
):
    rows, width = members.shape
    half = width // 2
    lists = n_list * LIST_DEV
    per_list = n_help // 2
    units = n_list * per_list
    i_list = lax.axis_index("list")
    i_help = lax.axis_index("help")
    core = lax.rem(i_help, 2)
    unit = i_list * per_list + i_help // 2

    def wrap(u):
        return jnp.where(u >= units, u - units, u)

    def device_of(u, c):
        return (u // per_list, lax.rem(u, per_list) * 2 + c)

    sibling = (i_list, i_help + 1 - 2 * core)

    load = pltpu.make_async_copy(source, members, load_sem)
    load.start()

    barrier = pltpu.get_barrier_semaphore()

    @pl.loop(1, units, unroll=3)
    def _(d):
        pl.semaphore_signal(
            barrier, inc=1, device_id=device_of(wrap(unit + d), core), device_id_type=MESH
        )

    for d in range(1, n_help):
        to = lax.rem(i_help + d, n_help)

        @pl.when(lax.rem(to, 2) != core)
        def _():
            pl.semaphore_signal(barrier, inc=1, device_id=(i_list, to), device_id_type=MESH)

    def arrive():
        load.wait()
        pl.semaphore_wait(barrier, units - 1 + per_list)

    def swap_copy(q):
        return pltpu.make_async_remote_copy(
            src_ref=acc.at[q, 1 - core], dst_ref=theirs.at[q],
            send_sem=sib_send.at[q], recv_sem=sib_recv.at[q],
            device_id=sibling, device_id_type=MESH,
        )

    def scatter(q):
        swap_copy(q).wait()
        part[q] = (acc[q, core] + theirs[q]).reshape(part.shape[1:])

        @pl.loop(1, units, unroll=3)
        def _(d):
            to = wrap(unit + d)
            pltpu.make_async_remote_copy(
                src_ref=part.at[q, to], dst_ref=gathered.at[q, unit],
                send_sem=rs_send.at[q], recv_sem=rs_recv.at[q],
                device_id=device_of(to, core), device_id_type=MESH,
            ).start()

        gathered[q, unit] = part[q, unit]

    def scatter_wait(q):
        pltpu.make_async_remote_copy(
            src_ref=part.at[q, : units - 1], dst_ref=gathered.at[q, : units - 1],
            send_sem=rs_send.at[q], recv_sem=rs_recv.at[q],
            device_id=sibling, device_id_type=MESH,
        ).wait()

    def half_logit(t, h):
        cols = pl.ds(pl.multiple_of(t * TILE, TILE), TILE)
        start = pl.multiple_of(h * half, LANES)
        inner = lax.dot_general(
            table[h], members[cols, pl.ds(start, half)], (((1,), (1,)), ((), ())),
            preferred_element_type=jnp.float32,
        )
        owner = jnp.broadcast_to(own[:, cols], (K, TILE))
        logit = jnp.zeros((K, TILE), jnp.float32)
        for l in range(lists):
            row = slice(l * K, (l + 1) * K)
            logit = jnp.where(owner == l, inner[row] - power[h, row, 0:1], logit)
        return logit

    def unpack(h):
        for l in range(lists):
            got = packs[h, l].astype(jnp.float32)
            got = jnp.concatenate([got[:K], got[K:]], axis=1)
            norm = jnp.sum(got[:, half:], axis=1, keepdims=True)
            power[h, l * K : (l + 1) * K, :] = jnp.broadcast_to(norm, (K, LANES))
            wide_table[l] = got[:, :half]
        table[h] = wide_table[...].reshape(table.shape[1:]).astype(jnp.bfloat16)

    def assign(t):
        cols = pl.ds(pl.multiple_of(t * TILE, TILE), TILE)
        logit = logits[:, cols] + half_logit(t, 1 - core)
        e = jnp.exp(logit - jnp.max(logit, axis=0, keepdims=True))
        return e / jnp.sum(e, axis=0, keepdims=True)

    def seeded(t):
        cols = pl.ds(pl.multiple_of(t * TILE, TILE), TILE)
        label = jnp.broadcast_to(seed[:, cols], (K, TILE))
        return jnp.where(label == lax.broadcasted_iota(jnp.int32, (K, TILE), 0), 1.0, 0.0)

    def weigh_all(weigh):
        count[...] = jnp.zeros_like(count)

        @pl.loop(0, rows // TILE)
        def _(t):
            cols = pl.ds(pl.multiple_of(t * TILE, TILE), TILE)
            weight = weigh(t).astype(jnp.bfloat16).astype(jnp.float32)
            owner = jnp.broadcast_to(own[:, cols], (K, TILE))
            spread = jnp.concatenate(
                [jnp.where(owner == l, weight, 0.0) for l in range(lists)], axis=0
            )
            weights[:, cols] = spread.astype(jnp.bfloat16)
            total = spread[:, :LANES]
            for j in range(1, TILE // LANES):
                total = total + spread[:, j * LANES : (j + 1) * LANES]
            count[...] += total

    def sum_columns(columns):
        return jnp.dot(weights[...], columns, preferred_element_type=jnp.float32)

    def exchange():
        ends = jnp.concatenate(
            [members[:, :LANES], members[:, half : half + LANES]], axis=1
        )
        sums = sum_columns(ends)
        for h in range(2):
            acc[0, h, :, :LANES] = sums[:, h * LANES : (h + 1) * LANES]
            acc[0, h, :, LANES:] = count[...]
        swap_copy(0).start()

        def rest(h):
            start = pl.multiple_of(h * half + LANES, LANES)
            acc[1, h] = sum_columns(members[:, pl.ds(start, half - LANES)])

        rest(1 - core)
        swap_copy(1).start()
        scatter(0)
        rest(core)
        scatter(1)
        scatter_wait(0)
        scatter_wait(1)

        block = [gathered[q, 0] for q in range(2)]
        for u in range(1, units):
            block = [block[q] + gathered[q, u] for q in range(2)]
        total = jnp.sum(block[0][:, LANES:], axis=1, keepdims=True)
        centers = jnp.concatenate([block[0][:, :LANES], block[1]], axis=1) / (total + 1.0)
        mine[...] = centers
        norm = 0.5 * jnp.sum(centers * centers, axis=1, keepdims=True)
        hi = norm.astype(jnp.bfloat16).astype(jnp.float32)
        mid = (norm - hi).astype(jnp.bfloat16).astype(jnp.float32)
        lo = norm - hi - mid
        lane = lax.broadcasted_iota(jnp.int32, (K, LANES), 1)
        tail = jnp.where(lane == 0, hi, jnp.where(lane == 1, mid, jnp.where(lane == 2, lo, 0.0)))
        wide = jnp.concatenate([centers, tail], axis=1)
        side = wide.shape[1] // 2
        packs[core, unit] = jnp.concatenate(
            [wide[:, :side], wide[:, side:]], axis=0
        ).astype(jnp.bfloat16)

        @pl.loop(1, units, unroll=3)
        def _(d):
            pltpu.make_async_remote_copy(
                src_ref=packs.at[core, unit], dst_ref=packs.at[core, unit],
                send_sem=ag_send.at[0], recv_sem=ag_recv.at[0],
                device_id=device_of(wrap(unit + d), core), device_id_type=MESH,
            ).start()

        pltpu.make_async_remote_copy(
            src_ref=packs.at[core, : units - 1], dst_ref=packs.at[core, : units - 1],
            send_sem=ag_send.at[0], recv_sem=ag_recv.at[0],
            device_id=sibling, device_id_type=MESH,
        ).wait()

        forward = pltpu.make_async_remote_copy(
            src_ref=packs.at[core], dst_ref=packs.at[core],
            send_sem=sib_send.at[2], recv_sem=sib_recv.at[2],
            device_id=sibling, device_id_type=MESH,
        )
        forward.start()

        unpack(core)

        @pl.loop(0, rows // TILE)
        def _(t):
            logits[:, pl.ds(pl.multiple_of(t * TILE, TILE), TILE)] = half_logit(t, core)

        forward.wait_send()
        pltpu.make_async_remote_copy(
            src_ref=packs.at[core], dst_ref=packs.at[1 - core],
            send_sem=sib_send.at[2], recv_sem=sib_recv.at[2],
            device_id=sibling, device_id_type=MESH,
        ).wait_recv()
        unpack(1 - core)

    weigh_all(seeded)
    arrive()
    exchange()

    @pl.loop(0, ITERS)
    def _(turn):
        weigh_all(assign)
        exchange()

    def fin_copy(d, slot):
        return pltpu.make_async_remote_copy(
            src_ref=mine, dst_ref=cent.at[slot],
            send_sem=fin_send.at[d], recv_sem=fin_recv.at[d],
            device_id=(i_list, lax.rem(i_help + d, n_help)), device_id_type=MESH,
        )

    for d in range(1, n_help):
        fin_copy(d, i_help).start()
    cent[i_help] = mine[...]

    @pl.loop(0, rows // TILE)
    def _(t):
        cols = pl.ds(pl.multiple_of(t * TILE, TILE), TILE)
        out[:, cols] = assign(t)

    for d in range(1, n_help):
        fin_copy(d, lax.rem(i_help + n_help - d, n_help)).wait()


def local(members, owner, seed_label):
    rows, width = members.shape
    n_list, n_help = lax.axis_size("list"), lax.axis_size("help")
    lists = n_list * LIST_DEV
    units = n_list * n_help // 2
    half = width // 2
    packed = half + LANES
    vmem = pl.BlockSpec(memory_space=pltpu.VMEM)
    dma = pltpu.SemaphoreType.DMA
    out, cent = pl.pallas_call(
        functools.partial(kernel, n_list, n_help),
        out_shape=(
            jax.ShapeDtypeStruct((K, rows), jnp.float32),
            jax.ShapeDtypeStruct((n_help, K, half), jnp.float32),
        ),
        in_specs=[pl.BlockSpec(memory_space=pl.ANY), vmem, vmem],
        out_specs=(vmem, vmem),
        scratch_shapes=[
            pltpu.VMEM((rows, width), jnp.bfloat16),
            pltpu.VMEM((lists * K, rows), jnp.bfloat16),
            pltpu.VMEM((lists * K, LANES), jnp.float32),
            pltpu.VMEM((2, 2, lists * K, half - LANES), jnp.float32),
            pltpu.VMEM((2, lists * K, half - LANES), jnp.float32),
            pltpu.VMEM((2, units, K, half - LANES), jnp.float32),
            pltpu.VMEM((2, units, K, half - LANES), jnp.float32),
            pltpu.VMEM((2, units, 2 * K, packed // 2), jnp.bfloat16),
            pltpu.VMEM((2, lists * K, half), jnp.bfloat16),
            pltpu.VMEM((2, lists * K, LANES), jnp.float32),
            pltpu.VMEM((K, half), jnp.float32),
            pltpu.VMEM((lists, K, half), jnp.float32),
            pltpu.VMEM((K, rows), jnp.float32),
            dma((3,)),
            dma((3,)),
            dma((2,)),
            dma((2,)),
            dma((1,)),
            dma((1,)),
            dma((n_help,)),
            dma((n_help,)),
            dma,
        ],
        compiler_params=pltpu.CompilerParams(
            collective_id=0, has_side_effects=True, vmem_limit_bytes=60 * 1024 * 1024
        ),
    )(members, owner.reshape(1, rows), seed_label.reshape(1, rows))
    cent = cent.reshape(n_help // 2, 2, K, half).transpose(0, 2, 1, 3)
    return out, cent.reshape(LIST_DEV, K, width)


def solution(mesh):
    placed = (P(("list", "help"), None), P(("list", "help"), None), P(("list", "help")))
    return jax.shard_map(
        local,
        mesh=mesh,
        in_specs=placed,
        out_specs=(P(None, ("list", "help")), P("list", None, None)),
        check_vma=False,
    )
```

```python
import functools
import jax
import jax.numpy as jnp
from jax import lax
from jax.experimental import pallas as pl
from jax.experimental.pallas import tpu as pltpu
from jax.sharding import PartitionSpec as P

K = 8
ITERS = 3
LIST_DEV = 2
TILE = 1024
LANES = 128
MESH = pl.DeviceIdType.MESH


def kernel(
    n_list, n_help, source, own, seed, out, cent,
    members, weights, count, acc, theirs, part, gathered, packs, table, power, mine, wide_table, logits,
    sib_send, sib_recv, rs_send, rs_recv, ag_send, ag_recv, fin_send, fin_recv, load_sem,
):
    rows, width = members.shape
    half = width // 2
    lists = n_list * LIST_DEV
    per_list = n_help // 2
    units = n_list * per_list
    i_list = lax.axis_index("list")
    i_help = lax.axis_index("help")
    core = lax.rem(i_help, 2)
    unit = i_list * per_list + i_help // 2

    def wrap(u):
        return jnp.where(u >= units, u - units, u)

    def device_of(u, c):
        return (u // per_list, lax.rem(u, per_list) * 2 + c)

    sibling = (i_list, i_help + 1 - 2 * core)

    load = pltpu.make_async_copy(source, members, load_sem)
    load.start()

    barrier = pltpu.get_barrier_semaphore()

    @pl.loop(1, units, unroll=3)
    def _(d):
        pl.semaphore_signal(
            barrier, inc=1, device_id=device_of(wrap(unit + d), core), device_id_type=MESH
        )

    for d in range(1, n_help):
        to = lax.rem(i_help + d, n_help)

        @pl.when(lax.rem(to, 2) != core)
        def _():
            pl.semaphore_signal(barrier, inc=1, device_id=(i_list, to), device_id_type=MESH)

    def arrive():
        load.wait()
        pl.semaphore_wait(barrier, units - 1 + per_list)

    def swap_copy(q):
        return pltpu.make_async_remote_copy(
            src_ref=acc.at[q, 1 - core], dst_ref=theirs.at[q],
            send_sem=sib_send.at[q], recv_sem=sib_recv.at[q],
            device_id=sibling, device_id_type=MESH,
        )

    def scatter(q):
        swap_copy(q).wait()
        part[q] = (acc[q, core] + theirs[q]).reshape(part.shape[1:])

        @pl.loop(1, units, unroll=3)
        def _(d):
            to = wrap(unit + d)
            pltpu.make_async_remote_copy(
                src_ref=part.at[q, to], dst_ref=gathered.at[q, unit],
                send_sem=rs_send.at[q], recv_sem=rs_recv.at[q],
                device_id=device_of(to, core), device_id_type=MESH,
            ).start()

        gathered[q, unit] = part[q, unit]

    def scatter_wait(q):
        pltpu.make_async_remote_copy(
            src_ref=part.at[q, : units - 1], dst_ref=gathered.at[q, : units - 1],
            send_sem=rs_send.at[q], recv_sem=rs_recv.at[q],
            device_id=sibling, device_id_type=MESH,
        ).wait()

    def half_logit(t, h):
        cols = pl.ds(pl.multiple_of(t * TILE, TILE), TILE)
        start = pl.multiple_of(h * half, LANES)
        inner = lax.dot_general(
            table[h], members[cols, pl.ds(start, half)], (((1,), (1,)), ((), ())),
            preferred_element_type=jnp.float32,
        )
        owner = jnp.broadcast_to(own[:, cols], (K, TILE))
        logit = jnp.zeros((K, TILE), jnp.float32)
        for l in range(lists):
            row = slice(l * K, (l + 1) * K)
            logit = jnp.where(owner == l, inner[row] - power[h, row, 0:1], logit)
        return logit

    def unpack(h):
        for l in range(lists):
            got = packs[h, l].astype(jnp.float32)
            got = jnp.concatenate([got[:K], got[K:]], axis=1)
            norm = jnp.sum(got[:, half:], axis=1, keepdims=True)
            power[h, l * K : (l + 1) * K, :] = jnp.broadcast_to(norm, (K, LANES))
            wide_table[l] = got[:, :half]
        table[h] = wide_table[...].reshape(table.shape[1:]).astype(jnp.bfloat16)

    def assign(t):
        cols = pl.ds(pl.multiple_of(t * TILE, TILE), TILE)
        logit = logits[:, cols] + half_logit(t, 1 - core)
        e = jnp.exp(logit - jnp.max(logit, axis=0, keepdims=True))
        return e / jnp.sum(e, axis=0, keepdims=True)

    def seeded(t):
        cols = pl.ds(pl.multiple_of(t * TILE, TILE), TILE)
        label = jnp.broadcast_to(seed[:, cols], (K, TILE))
        return jnp.where(label == lax.broadcasted_iota(jnp.int32, (K, TILE), 0), 1.0, 0.0)

    def weigh_all(weigh):
        count[...] = jnp.zeros_like(count)

        @pl.loop(0, rows // TILE)
        def _(t):
            cols = pl.ds(pl.multiple_of(t * TILE, TILE), TILE)
            weight = weigh(t).astype(jnp.bfloat16).astype(jnp.float32)
            owner = jnp.broadcast_to(own[:, cols], (K, TILE))
            spread = jnp.concatenate(
                [jnp.where(owner == l, weight, 0.0) for l in range(lists)], axis=0
            )
            weights[:, cols] = spread.astype(jnp.bfloat16)
            total = spread[:, :LANES]
            for j in range(1, TILE // LANES):
                total = total + spread[:, j * LANES : (j + 1) * LANES]
            count[...] += total

    def sum_columns(columns):
        return jnp.dot(weights[...], columns, preferred_element_type=jnp.float32)

    def exchange():
        ends = jnp.concatenate(
            [members[:, :LANES], members[:, half : half + LANES]], axis=1
        )
        sums = sum_columns(ends)
        for h in range(2):
            acc[0, h, :, :LANES] = sums[:, h * LANES : (h + 1) * LANES]
            acc[0, h, :, LANES:] = count[...]
        swap_copy(0).start()

        def rest(h):
            start = pl.multiple_of(h * half + LANES, LANES)
            acc[1, h] = sum_columns(members[:, pl.ds(start, half - LANES)])

        rest(1 - core)
        swap_copy(1).start()
        scatter(0)
        rest(core)
        scatter(1)
        scatter_wait(0)
        scatter_wait(1)

        block = [gathered[q, 0] for q in range(2)]
        for u in range(1, units):
            block = [block[q] + gathered[q, u] for q in range(2)]
        total = jnp.sum(block[0][:, LANES:], axis=1, keepdims=True)
        centers = jnp.concatenate([block[0][:, :LANES], block[1]], axis=1) / (total + 1.0)
        mine[...] = centers
        norm = 0.5 * jnp.sum(centers * centers, axis=1, keepdims=True)
        hi = norm.astype(jnp.bfloat16).astype(jnp.float32)
        mid = (norm - hi).astype(jnp.bfloat16).astype(jnp.float32)
        lo = norm - hi - mid
        lane = lax.broadcasted_iota(jnp.int32, (K, LANES), 1)
        tail = jnp.where(lane == 0, hi, jnp.where(lane == 1, mid, jnp.where(lane == 2, lo, 0.0)))
        wide = jnp.concatenate([centers, tail], axis=1)
        side = wide.shape[1] // 2
        packs[core, unit] = jnp.concatenate(
            [wide[:, :side], wide[:, side:]], axis=0
        ).astype(jnp.bfloat16)

        @pl.loop(1, units, unroll=3)
        def _(d):
            pltpu.make_async_remote_copy(
                src_ref=packs.at[core, unit], dst_ref=packs.at[core, unit],
                send_sem=ag_send.at[0], recv_sem=ag_recv.at[0],
                device_id=device_of(wrap(unit + d), core), device_id_type=MESH,
            ).start()

        pltpu.make_async_remote_copy(
            src_ref=packs.at[core, : units - 1], dst_ref=packs.at[core, : units - 1],
            send_sem=ag_send.at[0], recv_sem=ag_recv.at[0],
            device_id=sibling, device_id_type=MESH,
        ).wait()

        forward = pltpu.make_async_remote_copy(
            src_ref=packs.at[core], dst_ref=packs.at[core],
            send_sem=sib_send.at[2], recv_sem=sib_recv.at[2],
            device_id=sibling, device_id_type=MESH,
        )
        forward.start()

        unpack(core)

        @pl.loop(0, rows // TILE)
        def _(t):
            logits[:, pl.ds(pl.multiple_of(t * TILE, TILE), TILE)] = half_logit(t, core)

        forward.wait_send()
        pltpu.make_async_remote_copy(
            src_ref=packs.at[core], dst_ref=packs.at[1 - core],
            send_sem=sib_send.at[2], recv_sem=sib_recv.at[2],
            device_id=sibling, device_id_type=MESH,
        ).wait_recv()
        unpack(1 - core)

    weigh_all(seeded)
    arrive()
    exchange()

    @pl.loop(0, ITERS)
    def _(turn):
        weigh_all(assign)
        exchange()

    def fin_copy(d, slot):
        return pltpu.make_async_remote_copy(
            src_ref=mine, dst_ref=cent.at[slot],
            send_sem=fin_send.at[d], recv_sem=fin_recv.at[d],
            device_id=(i_list, lax.rem(i_help + d, n_help)), device_id_type=MESH,
        )

    for d in range(1, n_help):
        fin_copy(d, i_help).start()
    cent[i_help] = mine[...]

    @pl.loop(0, rows // TILE)
    def _(t):
        cols = pl.ds(pl.multiple_of(t * TILE, TILE), TILE)
        out[:, cols] = assign(t)

    for d in range(1, n_help):
        fin_copy(d, lax.rem(i_help + n_help - d, n_help)).wait()


def local(members, owner, seed_label):
    rows, width = members.shape
    n_list, n_help = lax.axis_size("list"), lax.axis_size("help")
    lists = n_list * LIST_DEV
    units = n_list * n_help // 2
    half = width // 2
    packed = half + LANES
    vmem = pl.BlockSpec(memory_space=pltpu.VMEM)
    dma = pltpu.SemaphoreType.DMA
    out, cent = pl.pallas_call(
        functools.partial(kernel, n_list, n_help),
        out_shape=(
            jax.ShapeDtypeStruct((K, rows), jnp.float32),
            jax.ShapeDtypeStruct((n_help, K, half), jnp.float32),
        ),
        in_specs=[pl.BlockSpec(memory_space=pl.ANY), vmem, vmem],
        out_specs=(vmem, vmem),
        scratch_shapes=[
            pltpu.VMEM((rows, width), jnp.bfloat16),
            pltpu.VMEM((lists * K, rows), jnp.bfloat16),
            pltpu.VMEM((lists * K, LANES), jnp.float32),
            pltpu.VMEM((2, 2, lists * K, half - LANES), jnp.float32),
            pltpu.VMEM((2, lists * K, half - LANES), jnp.float32),
            pltpu.VMEM((2, units, K, half - LANES), jnp.float32),
            pltpu.VMEM((2, units, K, half - LANES), jnp.float32),
            pltpu.VMEM((2, units, 2 * K, packed // 2), jnp.bfloat16),
            pltpu.VMEM((2, lists * K, half), jnp.bfloat16),
            pltpu.VMEM((2, lists * K, LANES), jnp.float32),
            pltpu.VMEM((K, half), jnp.float32),
            pltpu.VMEM((lists, K, half), jnp.float32),
            pltpu.VMEM((K, rows), jnp.float32),
            dma((3,)),
            dma((3,)),
            dma((2,)),
            dma((2,)),
            dma((1,)),
            dma((1,)),
            dma((n_help,)),
            dma((n_help,)),
            dma,
        ],
        compiler_params=pltpu.CompilerParams(
            collective_id=0, has_side_effects=True, vmem_limit_bytes=52 * 1024 * 1024
        ),
    )(members, owner.reshape(1, rows), seed_label.reshape(1, rows))
    cent = cent.reshape(n_help // 2, 2, K, half).transpose(0, 2, 1, 3)
    return out, cent.reshape(LIST_DEV, K, width)


def solution(mesh):
    placed = (P(("list", "help"), None), P(("list", "help"), None), P(("list", "help")))
    return jax.shard_map(
        local,
        mesh=mesh,
        in_specs=placed,
        out_specs=(P(None, ("list", "help")), P("list", None, None)),
        check_vma=False,
    )
```
